32 devices in a mesh: role: 4 (over y, x), section: 2 (over core), mp: 4 (over z).
Axes of the slice: x: 2, y: 2, z: 4, core: 2. Of those that a mesh axis runs over, the one named last changes fastest.
Arguments:
- states: bfloat16 [16, 64, 8192], P('role', None, 'mp'), may hold values from -6 to 6
- weights: bfloat16 [2, 8192, 8192], P('section', None, 'mp'), may hold values from -0.0625 to 0.0625
- head: bfloat16 [8192], P('mp'), may hold values from -0.0625 to 0.0625
- lengths: int32 [16], P('role'), may hold values from 1 to 64, as said below
- rewards: int32 [16], P('role'), may hold values from 0 to 1000
Outputs:
- weight_grads: bfloat16 [2, 8192, 8192], P('section', 'role', 'mp')
The draws below stay inside these ranges and needn't reach their ends.
Inputs may be any that keep to these rules, and one draw needn't show every extreme that they name: `lengths`: at least one dialogue fills all 64 slots.
All inputs are finite; a program needn't handle non-finite values.
Results may differ from the reference program's by a relative error of at most 0.014.
Values may be sent and summed in bfloat16 or wider, within the bound.
No kernel may reach another device: no remote copies, remote signals or barrier semaphores. Data moves between devices by JAX's collectives and lax.ppermute only.
A program may use at most 384 MiB of HBM per device.

```python
import jax
import jax.numpy as jnp
from jax import lax

D = 8192
DLG = 4
LEN = 64
MB = 4
DIALOGS = 16
N_ROLE = 4
N_SECTION = 2
N_MP = 4


def draw_lengths(key, part):
    first_key, second_key = jax.random.split(jax.random.fold_in(key, 7))
    base = jax.random.randint(first_key, (DIALOGS,), 1, LEN + 1)
    chosen = jax.random.randint(second_key, (), 0, DIALOGS)
    return jnp.where(jnp.arange(DIALOGS) == chosen, LEN, base).astype(jnp.int32)


def with_ends(values, rng, least, top_value):
    longest = values.shape.index(max(values.shape))
    spots = []
    for shift in (0, 1):
        where = [jax.random.randint(jax.random.fold_in(rng, axis), (), 0, length) for axis, length in enumerate(values.shape)]
        where[longest] = (where[longest] + shift) % values.shape[longest]
        spots.append(tuple(where))
    return values.at[spots[0]].set(least).at[spots[1]].set(top_value)


def steps_of(own_key, extent, pieces, low, top_value):
    def one(dim, parts):
        heights = jax.random.uniform(jax.random.fold_in(jax.random.fold_in(own_key, 6), dim), (parts,), jnp.float32, low / len(pieces), top_value / len(pieces))
        return jnp.repeat(jnp.exp(heights), extent[dim] // parts).reshape((-1,) + (1,) * (len(extent) - dim - 1))

    gain = one(*pieces[0])
    for cut in pieces[1:]:
        gain = gain * one(*cut)
    return gain


def gaussian(own_key, dims, scale, limit, shards=(), kind=jnp.bfloat16):
    gain = steps_of(own_key, dims, shards, -0.22, 0.18) if shards else 1.0
    drawn = jax.random.normal(own_key, dims, jnp.float32) * scale * gain
    return jnp.minimum(jnp.maximum(drawn, -limit), limit).astype(kind)


def setup_inputs(seed: int = 0) -> dict:
    seeds = jax.random.split(jax.random.key(seed), 6)
    states = gaussian(seeds[0], (DIALOGS, LEN, D), 1.0, 6.0, ((0, 4), (2, 4)))
    weights = gaussian(seeds[1], (N_SECTION, D, D), D ** -0.5, 0.0625, ((0, 2), (2, 4)))
    head = gaussian(seeds[2], (D,), D ** -0.5, 0.0625, ((0, 4),))
    lengths = draw_lengths(jax.random.fold_in(seeds[5], 71), 0)
    rewards = with_ends(jax.random.randint(seeds[4], (DIALOGS,), 0, 1001), jax.random.fold_in(seeds[4], 1), 0, 1000).astype(jnp.int32)
    return {"states": states, "weights": weights, "head": head, "lengths": lengths, "rewards": rewards}


GAMMA = 0.97


def silu_slope(z):
    sig = jax.nn.sigmoid(z)
    return sig * (1.0 + z * (1.0 - sig))


def targets_of(lengths, rewards, span):
    places = jnp.arange(span, dtype=jnp.int32)[None, :]
    live = places < lengths[:, None]
    mask = live.astype(jnp.float32)
    power = jnp.where(live, lengths[:, None] - 1 - places, 0).astype(jnp.float32)
    target = rewards.astype(jnp.float32)[:, None] / 1000.0 * jnp.power(jnp.float32(GAMMA), power) * mask
    return target.astype(jnp.bfloat16), mask


def reference(states, weights, head, lengths, rewards):
    share = DLG // N_ROLE
    block_rows = DLG * LEN // MB
    width = D // N_MP
    head_f = head.astype(jnp.float32)
    first_w = weights[0]
    second_w = weights[1]
    grad_first = jnp.zeros((D, D), jnp.float32)
    grad_second = jnp.zeros((D, D), jnp.float32)
    for owner in range(N_ROLE):
        picks = jnp.concatenate([group * DLG + owner * share + jnp.arange(share, dtype=jnp.int32) for group in range(N_ROLE)]).astype(jnp.int32)
        rows = states[picks].reshape(DLG * LEN, D)
        target, mask = targets_of(lengths[picks], rewards[picks], LEN)
        target = lax.optimization_barrier(target).astype(jnp.float32).reshape(-1)
        mask = mask.reshape(-1)
        for micro in range(MB):
            lo_row = micro * block_rows
            x = rows[lo_row:lo_row + block_rows]
            goal = target[lo_row:lo_row + block_rows]
            keep = mask[lo_row:lo_row + block_rows]
            z0 = jnp.dot(x, first_w, preferred_element_type=jnp.float32)
            y1 = (x.astype(jnp.float32) + jax.nn.silu(z0)).astype(jnp.bfloat16)
            z1 = jnp.dot(y1, second_w, preferred_element_type=jnp.float32)
            y2 = (y1.astype(jnp.float32) + jax.nn.silu(z1)).astype(jnp.bfloat16)
            value = jnp.dot(y2, head, preferred_element_type=jnp.float32)
            err = (value - goal) * keep
            dy2 = err[:, None] * head_f[None, :]
            dz1 = (dy2 * silu_slope(z1)).astype(jnp.bfloat16)
            blocks = jnp.einsum("rjc,djc->jrd", dz1.astype(jnp.float32).reshape(block_rows, N_MP, width), second_w.astype(jnp.float32).reshape(D, N_MP, width))
            blocks = lax.optimization_barrier(blocks.astype(jnp.bfloat16)).astype(jnp.float32)
            back1 = jnp.sum(blocks, axis=0)
            dx1 = (dy2 + back1).astype(jnp.bfloat16)
            dz0 = (dx1.astype(jnp.float32) * silu_slope(z0)).astype(jnp.bfloat16)
            grad_second = grad_second + jnp.dot(y1.T, dz1, preferred_element_type=jnp.float32)
            grad_first = grad_first + jnp.dot(x.T, dz0, preferred_element_type=jnp.float32)
    return jnp.stack([grad_first, grad_second]).astype(jnp.bfloat16)
```

```python
import jax
import jax.numpy as jnp
from jax import lax
from jax.experimental import pallas as pl
from jax.experimental.pallas import tpu as pltpu
from jax.sharding import PartitionSpec as P

GAMMA = 0.97
AXES = ("role", "section", "mp")


def silu_slope(z):
    sig = jax.nn.sigmoid(z)
    return sig * (1.0 + z * (1.0 - sig))


def targets_of(lengths, rewards, span):
    places = jnp.arange(span, dtype=jnp.int32)[None, :]
    live = places < lengths[:, None]
    mask = live.astype(jnp.float32)
    power = jnp.where(live, lengths[:, None] - 1 - places, 0).astype(jnp.float32)
    target = (
        rewards.astype(jnp.float32)[:, None] / 1000.0 * jnp.power(jnp.float32(GAMMA), power) * mask
    )
    return target.astype(jnp.bfloat16), mask


def mm(a, b, dims):
    return lax.dot_general(a, b, (dims, ((), ())), preferred_element_type=jnp.float32)


COST = pl.CostEstimate(flops=1024, bytes_accessed=1024, transcendentals=0)
ANYWHERE = pl.BlockSpec(memory_space=pl.ANY)
IN_VMEM = pl.BlockSpec(memory_space=pltpu.VMEM)
PARAMS = pltpu.CompilerParams(vmem_limit_bytes=40 * 1024 * 1024)


def flip_a(part):
    return jnp.where((part == 1) | (part == 2), 2, 1)


def weight_index(which, part):
    if which == "own":
        return part
    if which == "a":
        return part ^ flip_a(part)
    if which == "b":
        return part ^ (3 - flip_a(part))
    if which == "c":
        return part ^ 3
    return jnp.int32(which)


def block_matmul(act, weight, which, core, back=False, add=None, out=jnp.float32, other=None):
    rows, depth = act.shape
    height, cols = weight.shape[1:]
    width = height if back else cols
    tile = min(512, width)
    tiles = width // tile

    def kernel(*refs):
        refs = list(refs)
        act_ref = refs.pop(0)
        other_ref = refs.pop(0) if other is not None else None
        add_ref = refs.pop(0) if add is not None else None
        weight_ref, out_ref, left, extra, held, sems, act_sems = refs

        @pl.when(lax.axis_index("section") == core)
        def _():
            j = weight_index(which, lax.axis_index("mp"))

            def fetch(i):
                cut = pl.ds(pl.multiple_of(i * tile, tile), tile)
                part = weight_ref.at[j, cut, :] if back else weight_ref.at[j, :, cut]
                return pltpu.make_async_copy(part, held.at[i], sems.at[i])

            loads = [pltpu.make_async_copy(act_ref, left, act_sems.at[0])]
            if other_ref is not None:
                loads.append(pltpu.make_async_copy(other_ref, extra, act_sems.at[1]))
            for load in loads:
                load.start()
            for i in range(tiles):
                fetch(i).start()
            for load in loads:
                load.wait()
            if other_ref is not None:
                left[...] = left[...] + extra[...]

            def step(i, carry):
                fetch(i).wait()
                cut = pl.ds(pl.multiple_of(i * tile, tile), tile)
                term = mm(left[...], held[i], ((1,), (1,) if back else (0,)))
                if add_ref is not None:
                    term = term + add_ref[:, cut]
                out_ref[:, cut] = term.astype(out)
                return carry

            lax.fori_loop(0, tiles, step, 0)

    args = [act] + ([other] if other is not None else [])
    specs = [ANYWHERE] * len(args)
    if add is not None:
        args.append(add)
        specs.append(IN_VMEM)
    return pl.pallas_call(
        kernel,
        out_shape=jax.ShapeDtypeStruct((rows, width), out),
        in_specs=specs + [ANYWHERE],
        out_specs=IN_VMEM,
        scratch_shapes=[
            pltpu.VMEM((rows, depth), act.dtype),
            pltpu.VMEM((rows, depth) if other is not None else (16, 128), act.dtype),
            pltpu.VMEM((tiles, tile, cols) if back else (tiles, height, tile), weight.dtype),
            pltpu.SemaphoreType.DMA((tiles,)),
            pltpu.SemaphoreType.DMA((2,)),
        ],
        compiler_params=PARAMS,
        cost_estimate=COST,
        name="back_block" if back else "forward_block",
    )(*args, weight)


def pick_blocks(blocks, core):
    count = 4

    def kernel(*refs):
        given, taken, sems = refs[:5], refs[5:9], refs[-1]

        @pl.when(lax.axis_index("section") == core)
        def _():
            part, role = lax.axis_index("mp"), lax.axis_index("role")
            inner = (part == 1) | (part == 2)
            for k in range(count):
                d = part ^ role ^ k
                slot = jnp.where(inner & ((d == 1) | (d == 2)), 3 - d, d)
                slot = jnp.where((slot == 3) & ~inner, 4, slot)
                for j in range(5):

                    @pl.when(slot == j)
                    def _():
                        pltpu.make_async_copy(given[j], taken[k], sems.at[k]).start()

            for k in range(count):
                pltpu.make_async_copy(given[0], taken[k], sems.at[k]).wait()

    return pl.pallas_call(
        kernel,
        out_shape=[jax.ShapeDtypeStruct(blocks[0].shape, blocks[0].dtype)] * count,
        in_specs=[ANYWHERE] * 5,
        out_specs=[IN_VMEM] * count,
        scratch_shapes=[pltpu.SemaphoreType.DMA((count,))],
        compiler_params=PARAMS,
        cost_estimate=COST,
        name="pick_blocks",
    )(*blocks)


def per_device(states, weights, head, lengths, rewards):
    dialogs, span, width = states.shape
    roles, sections, parts = (lax.axis_size(a) for a in AXES)
    role, section, part = (lax.axis_index(a) for a in AXES)
    rows = dialogs * span
    model = weights.shape[1]
    weight = weights[0].reshape(parts, width, width)
    own_cols = model // roles
    line = parts == 4 and roles == 4
    tie = lax.optimization_barrier

    def place(r, s, m):
        return (r * sections + s) * parts + m

    def along(block, hops, source, target):
        return lax.ppermute(
            block,
            AXES,
            [(place(r, source, i), place(r, target, j)) for r in range(roles) for i, j in hops],
        )

    def across(block, flip, source, target):
        return lax.ppermute(
            block,
            AXES,
            [
                (place(r, source, m), place(r ^ flip, target, m))
                for r in range(roles)
                for m in range(parts)
            ],
        )

    round_a = [(0, 2), (3, 1), (1, 0), (2, 3)]
    round_b = [(2, 0), (1, 3), (0, 1), (3, 2)]
    ends_in, ends_out = [(1, 0), (2, 3)], [(0, 1), (3, 2)]
    middle = [(1, 2), (2, 1)]
    swap = [(m, m) for m in range(parts)]
    near = [(i, i ^ 1) for i in range(4)]
    far = [(i, i ^ 2) for i in range(4)]

    def times(block, which, core, add=None, other=None):
        return block_matmul(block, weight, which, core, add=add, other=other)

    def forward_all(own, core):
        whole = lax.all_gather(own, "mp")
        blocks = [whole[j] for j in range(parts)]
        total = None
        for j in range(parts):
            total = times(blocks[j], j, core, total)
        return total, blocks

    def columns_of(blocks):
        if line:
            return pick_blocks(blocks, 0)
        full = jnp.concatenate(blocks, axis=1)
        return [
            lax.dynamic_slice_in_dim(full, (role ^ k) * own_cols, own_cols, 1) for k in range(roles)
        ]

    def sum_parts(v, core):
        if not line:
            return lax.psum(v, "mp")
        v = v + along(v, near, core, core)
        return v + along(v, far, core, core)

    target, mask = targets_of(lengths, rewards, span)
    goal = target.astype(jnp.float32).reshape(rows)
    keep = mask.reshape(rows)
    head_f = head.astype(jnp.float32)
    x = states.reshape(rows, width)

    if line:
        a = along(x, round_a, 0, 0)
        z0 = times(x, "own", 0)
        own, z0 = tie((x, z0))
        b = along(own, round_b, 0, 0)
        passed = along(a, ends_in, 0, 0)
        own, a = tie((own, a))
        mid = along(own, middle, 0, 0)
        z0 = times(a, "a", 0, z0)
        z0 = times(b, "b", 0, z0)
        z0 = times(mid, "c", 0, z0, passed)
        blocks = [x, a, b, mid, passed]
    else:
        z0, blocks = forward_all(x, 0)
    y1 = (x.astype(jnp.float32) + jax.nn.silu(z0)).astype(jnp.bfloat16)
    slope = silu_slope(z0)

    if line:
        a = along(y1, round_a, 0, 0)
        here = along(y1, swap, 0, 1)
        z1 = times(here, "own", 1)
        own, z1 = tie((y1, z1))
        x_cols = columns_of(blocks)
        x_got = [x_cols[0]] + [across(x_cols[k], k, 0, 0) for k in (1, 2)]
        b = along(own, round_b, 0, 0)
        a, b, x_got = tie((a, b, x_got))
        passed = along(a, ends_in, 0, 0)
        own, a = tie((own, a))
        mid = along(own, middle, 0, 0)
        x_got.append(across(x_cols[3], 3, 0, 0))
        z1 = times(along(a, swap, 0, 1), "a", 1, z1)
        z1 = times(along(b, swap, 0, 1), "b", 1, z1)
        ends = [(0, 0), (3, 3)]
        inside = [(1, 1), (2, 2)]
        z1 = times(along(mid, inside, 0, 1), "c", 1, z1, along(passed, ends, 0, 1))
        blocks = [y1, a, b, mid, passed]
    else:
        here = jnp.where(section == 1, along(y1, swap, 0, 1), y1)
        x_cols = columns_of(blocks)
        x_got = [x_cols[0]] + [across(x_cols[k], k, 0, 0) for k in range(1, roles)]
        z1, blocks = forward_all(here, 1)

    blocks, x_got = tie((blocks, x_got))
    y_cols = columns_of(blocks)
    grad = (head_f[None, :] * silu_slope(z1)).astype(jnp.bfloat16)
    y2 = (here.astype(jnp.float32) + jax.nn.silu(z1)).astype(jnp.bfloat16)
    value = jnp.sum(y2.astype(jnp.float32) * head_f[None, :], axis=1)

    value, y_cols = tie((value, y_cols))
    y_got = [y_cols[0]] + [across(y_cols[k], k, 0, 0) for k in range(1, roles)]
    value = along(value, swap, 1, 0)
    grad_0 = along(grad, swap, 1, 0)

    def term(which, grad, out=jnp.bfloat16):
        return block_matmul(grad, weight, which, 1, True, None, out)

    if line:
        c = term("c", grad)
        passed = along(c, ends_out, 1, 1)
        mid = along(c, middle, 1, 1)
        grad, value, c = tie((grad, value, c))
        b = term("b", grad)
        got_b = along(b, round_a, 1, 1)
        grad, b, grad_0 = tie((grad, b, grad_0))
        a = term("a", grad, jnp.float32)
        a = (a + passed.astype(jnp.float32)).astype(jnp.bfloat16)
        a, y_got[1], y_got[2] = tie((a, y_got[1], y_got[2]))
        got_a = along(a, round_b, 1, 1)
        grad, a = tie((grad, a))
        own = term("own", grad, jnp.float32)
        back = own + (mid.astype(jnp.float32) + got_b.astype(jnp.float32))
        back = (back + got_a.astype(jnp.float32)).astype(jnp.bfloat16)
    else:
        whole = jnp.stack([term(j, grad) for j in range(parts)])
        whole = jnp.where(section == 1, whole, jnp.zeros_like(whole))
        back = lax.psum_scatter(whole, "mp", scatter_dimension=0)

    value = sum_parts(value, 0)
    err = (value - goal) * keep
    dz1 = (err[:, None] * grad_0.astype(jnp.float32)).astype(jnp.bfloat16)
    dz1_got = [dz1] + [across(dz1, k, 0, 0) for k in range(1, roles)]
    back, y_got, dz1_got[1], dz1_got[2] = tie((back, y_got, dz1_got[1], dz1_got[2]))
    back = along(back, swap, 1, 0)

    dx1 = err[:, None] * (head_f[None, :] + back.astype(jnp.float32))
    dx1 = dx1.astype(jnp.bfloat16).astype(jnp.float32)
    dz0 = (dx1 * slope).astype(jnp.bfloat16)
    dz0_got = [dz0] + [across(dz0, k, 0, 0) for k in range(1, roles)]
    y_got = [along(t, swap, 0, 1) for t in y_got]
    dz1_got = [along(t, swap, 0, 1) for t in dz1_got]

    def weight_grad(lefts, rights):
        left, right = jnp.concatenate(lefts, axis=0), jnp.concatenate(rights, axis=0)
        return mm(left, right, ((0,), (0,))).astype(jnp.bfloat16)

    grads = lax.cond(
        section == 1,
        lambda x, y, p, q: weight_grad(y, q),
        lambda x, y, p, q: weight_grad(x, p),
        x_got,
        y_got,
        dz0_got,
        dz1_got,
    )
    return grads[None]


def solution(mesh):
    placed = (P("role", None, "mp"), P("section", None, "mp"), P("mp"), P("role"), P("role"))
    return jax.shard_map(
        per_device,
        mesh=mesh,
        in_specs=placed,
        out_specs=P("section", "role", "mp"),
        check_vma=False,
    )
```

```python
import jax
import jax.numpy as jnp
from jax import lax
from jax.experimental import pallas as pl
from jax.experimental.pallas import tpu as pltpu
from jax.sharding import PartitionSpec as P

GAMMA = 0.97
AXES = ("role", "section", "mp")


def silu_slope(z):
    sig = jax.nn.sigmoid(z)
    return sig * (1.0 + z * (1.0 - sig))


def targets_of(lengths, rewards, span):
    places = jnp.arange(span, dtype=jnp.int32)[None, :]
    live = places < lengths[:, None]
    mask = live.astype(jnp.float32)
    power = jnp.where(live, lengths[:, None] - 1 - places, 0).astype(jnp.float32)
    target = (
        rewards.astype(jnp.float32)[:, None] / 1000.0 * jnp.power(jnp.float32(GAMMA), power) * mask
    )
    return target.astype(jnp.bfloat16), mask


def mm(a, b, dims):
    return lax.dot_general(a, b, (dims, ((), ())), preferred_element_type=jnp.float32)


COST = pl.CostEstimate(flops=1024, bytes_accessed=1024, transcendentals=0)
ANYWHERE = pl.BlockSpec(memory_space=pl.ANY)
IN_VMEM = pl.BlockSpec(memory_space=pltpu.VMEM)
PARAMS = pltpu.CompilerParams(vmem_limit_bytes=40 * 1024 * 1024)


def flip_a(part):
    return jnp.where((part == 1) | (part == 2), 2, 1)


def weight_index(which, part):
    if which == "own":
        return part
    if which == "a":
        return part ^ flip_a(part)
    if which == "b":
        return part ^ (3 - flip_a(part))
    if which == "c":
        return part ^ 3
    return jnp.int32(which)


def block_matmul(act, weight, which, core, back=False, add=None, out=jnp.float32, other=None):
    rows, depth = act.shape
    height, cols = weight.shape[1:]
    width = height if back else cols
    tile = min(512, width)
    tiles = width // tile

    def kernel(*refs):
        refs = list(refs)
        act_ref = refs.pop(0)
        other_ref = refs.pop(0) if other is not None else None
        add_ref = refs.pop(0) if add is not None else None
        weight_ref, out_ref, left, extra, held, sems, act_sems = refs

        @pl.when(lax.axis_index("section") == core)
        def _():
            j = weight_index(which, lax.axis_index("mp"))

            def fetch(i):
                cut = pl.ds(pl.multiple_of(i * tile, tile), tile)
                part = weight_ref.at[j, cut, :] if back else weight_ref.at[j, :, cut]
                return pltpu.make_async_copy(part, held.at[i], sems.at[i])

            loads = [pltpu.make_async_copy(act_ref, left, act_sems.at[0])]
            if other_ref is not None:
                loads.append(pltpu.make_async_copy(other_ref, extra, act_sems.at[1]))
            for load in loads:
                load.start()
            for i in range(tiles):
                fetch(i).start()
            for load in loads:
                load.wait()
            if other_ref is not None:
                left[...] = left[...] + extra[...]

            def step(i, carry):
                fetch(i).wait()
                cut = pl.ds(pl.multiple_of(i * tile, tile), tile)
                term = mm(left[...], held[i], ((1,), (1,) if back else (0,)))
                if add_ref is not None:
                    term = term + add_ref[:, cut]
                out_ref[:, cut] = term.astype(out)
                return carry

            lax.fori_loop(0, tiles, step, 0)

    args = [act] + ([other] if other is not None else [])
    specs = [ANYWHERE] * len(args)
    if add is not None:
        args.append(add)
        specs.append(IN_VMEM)
    return pl.pallas_call(
        kernel,
        out_shape=jax.ShapeDtypeStruct((rows, width), out),
        in_specs=specs + [ANYWHERE],
        out_specs=IN_VMEM,
        scratch_shapes=[
            pltpu.VMEM((rows, depth), act.dtype),
            pltpu.VMEM((rows, depth) if other is not None else (16, 128), act.dtype),
            pltpu.VMEM((tiles, tile, cols) if back else (tiles, height, tile), weight.dtype),
            pltpu.SemaphoreType.DMA((tiles,)),
            pltpu.SemaphoreType.DMA((2,)),
        ],
        compiler_params=PARAMS,
        cost_estimate=COST,
        name="back_block" if back else "forward_block",
    )(*args, weight)


def pick_blocks(blocks, core, count=4):

    def kernel(*refs):
        given, taken = refs[:5], refs[5 : 5 + count]
        held, sems, out_sems = refs[5 + count :]

        def leave(k):
            return pltpu.make_async_copy(held.at[k], taken[k], out_sems.at[k])

        @pl.when(lax.axis_index("section") == core)
        def _():
            part, role = lax.axis_index("mp"), lax.axis_index("role")
            inner = (part == 1) | (part == 2)
            for k in range(count):
                d = part ^ role ^ k
                slot = jnp.where(inner & ((d == 1) | (d == 2)), 3 - d, d)
                slot = jnp.where((slot == 3) & ~inner, 4, slot)
                for j in range(5):

                    @pl.when(slot == j)
                    def _():
                        pltpu.make_async_copy(given[j], held.at[k], sems.at[k]).start()

            for k in range(count):
                pltpu.make_async_copy(given[0], held.at[k], sems.at[k]).wait()
                leave(k).start()
            for k in range(count):
                leave(k).wait()

    return pl.pallas_call(
        kernel,
        out_shape=[jax.ShapeDtypeStruct(blocks[0].shape, blocks[0].dtype)] * count,
        in_specs=[ANYWHERE] * 5,
        out_specs=[ANYWHERE] * count,
        scratch_shapes=[
            pltpu.VMEM((count, *blocks[0].shape), blocks[0].dtype),
            pltpu.SemaphoreType.DMA((count,)),
            pltpu.SemaphoreType.DMA((count,)),
        ],
        compiler_params=PARAMS,
        cost_estimate=COST,
        name="pick_blocks",
    )(*blocks)


def per_device(states, weights, head, lengths, rewards):
    dialogs, span, width = states.shape
    roles, sections, parts = (lax.axis_size(a) for a in AXES)
    role, section, part = (lax.axis_index(a) for a in AXES)
    rows = dialogs * span
    model = weights.shape[1]
    weight = weights[0].reshape(parts, width, width)
    own_cols = model // roles
    line = parts == 4 and roles == 4
    tie = lax.optimization_barrier

    def place(r, s, m):
        return (r * sections + s) * parts + m

    def along(block, hops, source, target):
        return lax.ppermute(
            block,
            AXES,
            [(place(r, source, i), place(r, target, j)) for r in range(roles) for i, j in hops],
        )

    def across(block, flip, source, target):
        return lax.ppermute(
            block,
            AXES,
            [
                (place(r, source, m), place(r ^ flip, target, m))
                for r in range(roles)
                for m in range(parts)
            ],
        )

    round_a = [(0, 2), (3, 1), (1, 0), (2, 3)]
    round_b = [(2, 0), (1, 3), (0, 1), (3, 2)]
    ends_in = [(1, 0), (2, 3)]
    middle = [(1, 2), (2, 1)]
    opposite = [(i, i ^ 3) for i in range(4)]
    swap = [(m, m) for m in range(parts)]
    near = [(i, i ^ 1) for i in range(4)]
    far = [(i, i ^ 2) for i in range(4)]

    def times(block, which, core, add=None, other=None):
        return block_matmul(block, weight, which, core, add=add, other=other)

    def forward_all(own, core):
        whole = lax.all_gather(own, "mp")
        blocks = [whole[j] for j in range(parts)]
        total = None
        for j in range(parts):
            total = times(blocks[j], j, core, total)
        return total, blocks

    def columns_of(blocks):
        if line:
            return pick_blocks(blocks, 0)
        full = jnp.concatenate(blocks, axis=1)
        return [
            lax.dynamic_slice_in_dim(full, (role ^ k) * own_cols, own_cols, 1) for k in range(roles)
        ]

    def sum_parts(v, core):
        if not line:
            return lax.psum(v, "mp")
        v = v + along(v, near, core, core)
        return v + along(v, far, core, core)

    target, mask = targets_of(lengths, rewards, span)
    goal = target.astype(jnp.float32).reshape(rows)
    keep = mask.reshape(rows)
    head_f = head.astype(jnp.float32)
    x = states.reshape(rows, width)

    if line:
        a = along(x, round_a, 0, 0)
        z0 = times(x, "own", 0)
        own, z0 = tie((x, z0))
        b = along(own, round_b, 0, 0)
        passed = along(a, ends_in, 0, 0)
        own, a = tie((own, a))
        mid = along(own, middle, 0, 0)
        z0 = times(a, "a", 0, z0)
        z0 = times(b, "b", 0, z0)
        z0 = times(mid, "c", 0, z0, passed)
        blocks = [x, a, b, mid, passed]
    else:
        z0, blocks = forward_all(x, 0)
    y1 = (x.astype(jnp.float32) + jax.nn.silu(z0)).astype(jnp.bfloat16)
    slope = silu_slope(z0)

    if line:
        a = along(y1, round_a, 0, 0)
        here = along(y1, swap, 0, 1)
        z1 = times(here, "own", 1)
        own, z1 = tie((y1, z1))
        x_cols = columns_of(blocks)
        x_got = [x_cols[0]] + [across(x_cols[k], k, 0, 0) for k in (1, 2)]
        b = along(own, round_b, 0, 0)
        a, b, x_got = tie((a, b, x_got))
        passed = along(a, ends_in, 0, 0)
        own, a = tie((own, a))
        mid = along(own, middle, 0, 0)
        x_got.append(across(x_cols[3], 3, 0, 0))
        here_a, here_b = along(a, swap, 0, 1), along(b, swap, 0, 1)
        z1 = times(here_a, "a", 1, z1)
        z1 = times(here_b, "b", 1, z1)
        here_mid = along(mid, [(1, 1), (2, 2)], 0, 1)
        here_passed = along(passed, [(0, 0), (3, 3)], 0, 1)
        z1 = times(here_mid, "c", 1, z1, here_passed)
        blocks = [y1, a, b, mid, passed]
    else:
        here = jnp.where(section == 1, along(y1, swap, 0, 1), y1)
        x_cols = columns_of(blocks)
        x_got = [x_cols[0]] + [across(x_cols[k], k, 0, 0) for k in range(1, roles)]
        z1, blocks = forward_all(here, 1)

    y_cols = columns_of(blocks)
    if line:
        y_own = pick_blocks([here, here_a, here_b, here_mid, here_passed], 1, 1)[0]
        z1, y_own = tie((z1, y_own))
    else:
        y_own = y_cols[0]
    grad = (head_f[None, :] * silu_slope(z1)).astype(jnp.bfloat16)
    y2 = (here.astype(jnp.float32) + jax.nn.silu(z1)).astype(jnp.bfloat16)
    value = jnp.sum(y2.astype(jnp.float32) * head_f[None, :], axis=1)

    y_cols, x_got = tie((y_cols, x_got))
    def term(which, grad, out=jnp.bfloat16):
        return block_matmul(grad, weight, which, 1, True, None, out)

    if line:
        c = term("c", grad)
        grad, value, y_cols, c = tie((grad, value, y_cols, c))
    y_got = [y_own] + [across(y_cols[k], k, 0, 1) for k in range(1, roles)]
    value = along(value, swap, 1, 0)
    grad_0 = along(grad, swap, 1, 0)

    if line:
        got_c = along(c, opposite, 1, 1)
        b = term("b", grad)
        got_b = along(b, round_a, 1, 1)
        grad, b, grad_0 = tie((grad, b, grad_0))
        a = term("a", grad)
        got_a = along(a, round_b, 1, 1)
        value = sum_parts(value, 0)
        grad, a, got_c, value, y_got[1:3] = tie((grad, a, got_c, value, y_got[1:3]))
        own = term("own", grad, jnp.float32)
        back = own + (got_c.astype(jnp.float32) + got_b.astype(jnp.float32))
        back = (back + got_a.astype(jnp.float32)).astype(jnp.bfloat16)
    else:
        value = sum_parts(value, 0)
        whole = jnp.stack([term(j, grad) for j in range(parts)])
        whole = jnp.where(section == 1, whole, jnp.zeros_like(whole))
        back = lax.psum_scatter(whole, "mp", scatter_dimension=0)

    err = (value - goal) * keep
    dz1 = (err[:, None] * grad_0.astype(jnp.float32)).astype(jnp.bfloat16)
    dz1_got = [across(dz1, k, 0, 1) for k in (1, 2)]
    back, y_got[1:], dz1_got = tie((back, y_got[1:], dz1_got))
    back = along(back, swap, 1, 0)

    dx1 = err[:, None] * (head_f[None, :] + back.astype(jnp.float32))
    dx1 = dx1.astype(jnp.bfloat16).astype(jnp.float32)
    dz0 = (dx1 * slope).astype(jnp.bfloat16)
    dz0, dz1, err = tie((dz0, dz1, err))
    dz1_got.append(across(dz1, 3, 0, 1))
    err = along(err, swap, 0, 1)
    dz1_got.insert(0, (err[:, None] * grad.astype(jnp.float32)).astype(jnp.bfloat16))
    dz0_got = [dz0] + [across(dz0, k, 0, 0) for k in range(1, roles)]

    def own_of(zeroth, first):
        return jnp.concatenate([jnp.where(section == 1, f, z) for z, f in zip(zeroth, first)], axis=0)

    left, right = own_of(x_got, y_got), own_of(dz0_got, dz1_got)
    grads = mm(left, right, ((0,), (0,))).astype(jnp.bfloat16)
    return grads[None]


def solution(mesh):
    placed = (P("role", None, "mp"), P("section", None, "mp"), P("mp"), P("role"), P("role"))
    return jax.shard_map(
        per_device,
        mesh=mesh,
        in_specs=placed,
        out_specs=P("section", "role", "mp"),
        check_vma=False,
    )
```

```python
import jax
import jax.numpy as jnp
from jax import lax
from jax.experimental import pallas as pl
from jax.experimental.pallas import tpu as pltpu
from jax.sharding import PartitionSpec as P

GAMMA = 0.97
AXES = ("role", "section", "mp")


def silu_slope(z):
    sig = jax.nn.sigmoid(z)
    return sig * (1.0 + z * (1.0 - sig))


def targets_of(lengths, rewards, span):
    places = jnp.arange(span, dtype=jnp.int32)[None, :]
    live = places < lengths[:, None]
    mask = live.astype(jnp.float32)
    power = jnp.where(live, lengths[:, None] - 1 - places, 0).astype(jnp.float32)
    target = (
        rewards.astype(jnp.float32)[:, None] / 1000.0 * jnp.power(jnp.float32(GAMMA), power) * mask
    )
    return target.astype(jnp.bfloat16), mask


def mm(a, b, dims):
    return lax.dot_general(a, b, (dims, ((), ())), preferred_element_type=jnp.float32)


COST = pl.CostEstimate(flops=2 * 10**9, bytes_accessed=10**7, transcendentals=0)
ANYWHERE = pl.BlockSpec(memory_space=pl.ANY)
IN_VMEM = pl.BlockSpec(memory_space=pltpu.VMEM)
PARAMS = pltpu.CompilerParams(vmem_limit_bytes=40 * 1024 * 1024)


def flip_a(part):
    return jnp.where((part == 1) | (part == 2), 2, 1)


def weight_index(which, part):
    if which == "own":
        return part
    if which == "a":
        return part ^ flip_a(part)
    if which == "b":
        return part ^ (3 - flip_a(part))
    if which == "c":
        return part ^ 3
    return jnp.int32(which)


def block_matmul(act, weight, which, core, back=False, add=None, out=jnp.float32, other=None):
    rows, depth = act.shape
    height, cols = weight.shape[1:]
    width = height if back else cols
    tile = min(1024, width)
    tiles = width // tile

    def kernel(*refs):
        refs = list(refs)
        act_ref = refs.pop(0)
        other_ref = refs.pop(0) if other is not None else None
        add_ref = refs.pop(0) if add is not None else None
        weight_ref, out_ref, left, extra, held, sems, act_sems = refs

        @pl.when(lax.axis_index("section") == core)
        def _():
            j = weight_index(which, lax.axis_index("mp"))

            def fetch(i):
                cut = pl.ds(pl.multiple_of(i * tile, tile), tile)
                part = weight_ref.at[j, cut, :] if back else weight_ref.at[j, :, cut]
                return pltpu.make_async_copy(part, held.at[i], sems.at[i])

            loads = [pltpu.make_async_copy(act_ref, left, act_sems.at[0])]
            if other_ref is not None:
                loads.append(pltpu.make_async_copy(other_ref, extra, act_sems.at[1]))
            for load in loads:
                load.start()
            for i in range(tiles):
                fetch(i).start()
            for load in loads:
                load.wait()
            if other_ref is not None:
                left[...] = left[...] + extra[...]

            def step(i, carry):
                fetch(i).wait()
                cut = pl.ds(pl.multiple_of(i * tile, tile), tile)
                term = mm(left[...], held[i], ((1,), (1,) if back else (0,)))
                if add_ref is not None:
                    term = term + add_ref[:, cut]
                out_ref[:, cut] = term.astype(out)
                return carry

            lax.fori_loop(0, tiles, step, 0)

    args = [act] + ([other] if other is not None else [])
    specs = [ANYWHERE] * len(args)
    if add is not None:
        args.append(add)
        specs.append(IN_VMEM)
    return pl.pallas_call(
        kernel,
        out_shape=jax.ShapeDtypeStruct((rows, width), out),
        in_specs=specs + [ANYWHERE],
        out_specs=IN_VMEM,
        scratch_shapes=[
            pltpu.VMEM((rows, depth), act.dtype),
            pltpu.VMEM((rows, depth) if other is not None else (16, 128), act.dtype),
            pltpu.VMEM((tiles, tile, cols) if back else (tiles, height, tile), weight.dtype),
            pltpu.SemaphoreType.DMA((tiles,)),
            pltpu.SemaphoreType.DMA((2,)),
        ],
        compiler_params=PARAMS,
        cost_estimate=COST,
        name="back_block" if back else "forward_block",
    )(*args, weight)


def pick_blocks(blocks, core, count=4):

    def kernel(*refs):
        given, taken = refs[:5], refs[5 : 5 + count]
        held, sems, out_sems = refs[5 + count :]

        def leave(k):
            return pltpu.make_async_copy(held.at[k], taken[k], out_sems.at[k])

        @pl.when(lax.axis_index("section") == core)
        def _():
            part, role = lax.axis_index("mp"), lax.axis_index("role")
            inner = (part == 1) | (part == 2)
            for k in range(count):
                d = part ^ role ^ k
                slot = jnp.where(inner & ((d == 1) | (d == 2)), 3 - d, d)
                slot = jnp.where((slot == 3) & ~inner, 4, slot)
                for j in range(5):

                    @pl.when(slot == j)
                    def _():
                        pltpu.make_async_copy(given[j], held.at[k], sems.at[k]).start()

            for k in range(count):
                pltpu.make_async_copy(given[0], held.at[k], sems.at[k]).wait()
                leave(k).start()
            for k in range(count):
                leave(k).wait()

    return pl.pallas_call(
        kernel,
        out_shape=[jax.ShapeDtypeStruct(blocks[0].shape, blocks[0].dtype)] * count,
        in_specs=[ANYWHERE] * 5,
        out_specs=[ANYWHERE] * count,
        scratch_shapes=[
            pltpu.VMEM((count, *blocks[0].shape), blocks[0].dtype),
            pltpu.SemaphoreType.DMA((count,)),
            pltpu.SemaphoreType.DMA((count,)),
        ],
        compiler_params=PARAMS,
        cost_estimate=COST,
        name="pick_blocks",
    )(*blocks)


def per_device(states, weights, head, lengths, rewards):
    dialogs, span, width = states.shape
    roles, sections, parts = (lax.axis_size(a) for a in AXES)
    role, section, part = (lax.axis_index(a) for a in AXES)
    rows = dialogs * span
    model = weights.shape[1]
    weight = weights[0].reshape(parts, width, width)
    own_cols = model // roles
    line = parts == 4 and roles == 4
    tie = lax.optimization_barrier

    def place(r, s, m):
        return (r * sections + s) * parts + m

    def along(block, hops, source, target):
        return lax.ppermute(
            block,
            AXES,
            [(place(r, source, i), place(r, target, j)) for r in range(roles) for i, j in hops],
        )

    def across(block, flip, source, target):
        return lax.ppermute(
            block,
            AXES,
            [
                (place(r, source, m), place(r ^ flip, target, m))
                for r in range(roles)
                for m in range(parts)
            ],
        )

    round_a = [(0, 2), (3, 1), (1, 0), (2, 3)]
    round_b = [(2, 0), (1, 3), (0, 1), (3, 2)]
    ends_in = [(1, 0), (2, 3)]
    middle = [(1, 2), (2, 1)]
    opposite = [(i, i ^ 3) for i in range(4)]
    swap = [(m, m) for m in range(parts)]
    near = [(i, i ^ 1) for i in range(4)]
    far = [(i, i ^ 2) for i in range(4)]

    def times(block, which, core, add=None, other=None):
        return block_matmul(block, weight, which, core, add=add, other=other)

    def forward_all(own, core):
        whole = lax.all_gather(own, "mp")
        blocks = [whole[j] for j in range(parts)]
        total = None
        for j in range(parts):
            total = times(blocks[j], j, core, total)
        return total, blocks

    def columns_of(blocks):
        if line:
            return pick_blocks(blocks, 0)
        full = jnp.concatenate(blocks, axis=1)
        return [
            lax.dynamic_slice_in_dim(full, (role ^ k) * own_cols, own_cols, 1) for k in range(roles)
        ]

    def sum_parts(v, core):
        if not line:
            return lax.psum(v, "mp")
        v = v + along(v, near, core, core)
        return v + along(v, far, core, core)

    target, mask = targets_of(lengths, rewards, span)
    goal = target.astype(jnp.float32).reshape(rows)
    keep = mask.reshape(rows)
    head_f = head.astype(jnp.float32)
    x = states.reshape(rows, width)

    if line:
        a = along(x, round_a, 0, 0)
        z0 = times(x, "own", 0)
        own, z0 = tie((x, z0))
        b = along(own, round_b, 0, 0)
        passed = along(a, ends_in, 0, 0)
        own, a = tie((own, a))
        mid = along(own, middle, 0, 0)
        z0 = times(a, "a", 0, z0)
        z0 = times(b, "b", 0, z0)
        z0 = times(mid, "c", 0, z0, passed)
        blocks = [x, a, b, mid, passed]
    else:
        z0, blocks = forward_all(x, 0)
    y1 = (x.astype(jnp.float32) + jax.nn.silu(z0)).astype(jnp.bfloat16)
    slope = silu_slope(z0)

    if line:
        a = along(y1, round_a, 0, 0)
        here = along(y1, swap, 0, 1)
        z1 = times(here, "own", 1)
        own, z1 = tie((y1, z1))
        x_cols = columns_of(blocks)
        x_got = [x_cols[0]] + [across(x_cols[k], k, 0, 0) for k in (1, 2)]
        b = along(own, round_b, 0, 0)
        a, b, x_got = tie((a, b, x_got))
        passed = along(a, ends_in, 0, 0)
        own, a = tie((own, a))
        mid = along(own, middle, 0, 0)
        x_got.append(across(x_cols[3], 3, 0, 0))
        here_a, here_b = along(a, swap, 0, 1), along(b, swap, 0, 1)
        z1 = times(here_a, "a", 1, z1)
        z1 = times(here_b, "b", 1, z1)
        here_mid = along(mid, [(1, 1), (2, 2)], 0, 1)
        here_passed = along(passed, [(0, 0), (3, 3)], 0, 1)
        z1 = times(here_mid, "c", 1, z1, here_passed)
        blocks = [y1, a, b, mid, passed]
    else:
        here = jnp.where(section == 1, along(y1, swap, 0, 1), y1)
        x_cols = columns_of(blocks)
        x_got = [x_cols[0]] + [across(x_cols[k], k, 0, 0) for k in range(1, roles)]
        z1, blocks = forward_all(here, 1)

    y_cols = columns_of(blocks)
    if line:
        y_own = pick_blocks([here, here_a, here_b, here_mid, here_passed], 1, 1)[0]
        z1, y_own = tie((z1, y_own))
    else:
        y_own = y_cols[0]
    grad = (head_f[None, :] * silu_slope(z1)).astype(jnp.bfloat16)
    y2 = (here.astype(jnp.float32) + jax.nn.silu(z1)).astype(jnp.bfloat16)
    value = jnp.sum(y2.astype(jnp.float32) * head_f[None, :], axis=1)

    y_cols, x_got = tie((y_cols, x_got))
    def term(which, grad, out=jnp.bfloat16):
        return block_matmul(grad, weight, which, 1, True, None, out)

    if line:
        c = term("c", grad)
        grad, value, y_cols, c = tie((grad, value, y_cols, c))
    y_got = [y_own] + [across(y_cols[k], k, 0, 1) for k in range(1, roles)]
    value = along(value, swap, 1, 0)
    grad_0 = along(grad, swap, 1, 0)

    if line:
        got_c = along(c, opposite, 1, 1)
        b = term("b", grad)
        got_b = along(b, round_a, 1, 1)
        grad, b, grad_0 = tie((grad, b, grad_0))
        a = term("a", grad)
        got_a = along(a, round_b, 1, 1)
        value = sum_parts(value, 0)
        grad, a, got_c, value, y_got[1:3] = tie((grad, a, got_c, value, y_got[1:3]))
        own = term("own", grad, jnp.float32)
        back = own + (got_c.astype(jnp.float32) + got_b.astype(jnp.float32))
        back = (back + got_a.astype(jnp.float32)).astype(jnp.bfloat16)
    else:
        value = sum_parts(value, 0)
        whole = jnp.stack([term(j, grad) for j in range(parts)])
        whole = jnp.where(section == 1, whole, jnp.zeros_like(whole))
        back = lax.psum_scatter(whole, "mp", scatter_dimension=0)

    err = (value - goal) * keep
    dz1 = (err[:, None] * grad_0.astype(jnp.float32)).astype(jnp.bfloat16)
    dz1_got = [across(dz1, k, 0, 1) for k in (1, 2)]
    back, y_got[1:], dz1_got = tie((back, y_got[1:], dz1_got))
    back = along(back, swap, 1, 0)

    dx1 = err[:, None] * (head_f[None, :] + back.astype(jnp.float32))
    dx1 = dx1.astype(jnp.bfloat16).astype(jnp.float32)
    dz0 = (dx1 * slope).astype(jnp.bfloat16)
    dz0, dz1, err = tie((dz0, dz1, err))
    dz1_got.append(across(dz1, 3, 0, 1))
    err = along(err, swap, 0, 1)
    dz1_got.insert(0, (err[:, None] * grad.astype(jnp.float32)).astype(jnp.bfloat16))
    dz0_got = [dz0] + [across(dz0, k, 0, 0) for k in range(1, roles)]

    def own_of(zeroth, first):
        return jnp.concatenate([jnp.where(section == 1, f, z) for z, f in zip(zeroth, first)], axis=0)

    left, right = own_of(x_got, y_got), own_of(dz0_got, dz1_got)
    grads = mm(left, right, ((0,), (0,))).astype(jnp.bfloat16)
    return grads[None]


def solution(mesh):
    placed = (P("role", None, "mp"), P("section", None, "mp"), P("mp"), P("role"), P("role"))
    return jax.shard_map(
        per_device,
        mesh=mesh,
        in_specs=placed,
        out_specs=P("section", "role", "mp"),
        check_vma=False,
    )
```
